32 devices in a mesh: groups: 2 (over y), tile: 8 (over z, x), feat: 2 (over core).
Axes of the slice: x: 2, y: 2, z: 4, core: 2. Of those that a mesh axis runs over, the one named last changes fastest.
Arguments:
- preacts: bfloat16 [3, 16384, 256], P(None, ('tile', 'feat'), 'groups'), parts along dimension 2, may hold values from -6 to 6
- targets: bfloat16 [3, 512, 1152], P(None, ('groups', 'tile', 'feat')), parts along dimension 1, may hold values from -4 to 4
- decoder: bfloat16 [16, 2, 12288, 2304], P(('groups', 'tile'), 'feat'), parts along dimension 0, may hold values from -0.02734375 to 0.02734375
- owner_list: int32 [16384, 6, 1], P(('tile', 'feat')), may hold values from 0 to 7; in each aligned block of 6144 rows (0 to 6143, 6144 to 12287, ..., all dimensions but the last counted through in order) at most 1536 rows name the same one
- tile_source: int32 [6], replicated, may hold values from 0 to 2, as said below
- tile_target: int32 [6], replicated, may hold values from 0 to 2, as said below
- row_order: int32 [4, 64], P('groups'), parts along dimension 0, may hold values from 0 to 63, each once within a row
Outputs:
- residual: float32 [3, 512, 1152], P(None, ('groups', 'tile', 'feat')), parts along dimension 1
- feature_grad: float32 [3, 16384, 256], P(None, ('tile', 'feat'), 'groups'), parts along dimension 2
The draws below stay inside these ranges and needn't reach their ends.
There are 2 independent parts, one for each index of `groups`. The reference program is written for one: setup_inputs(seed, part) draws one part's arguments, and reference() takes and returns one part's arrays. A program takes and returns all parts, laid end to end along the dimension named above; an argument that names none is the same for every part. Nothing has to cross between parts.
Inputs may be any that keep to these rules, and one draw needn't show every extreme that they name: `owner_list`: among the 6144 rows of one device (features f with f // 1024 equal, all tiles), no owner is named more than 1536 times, and in some device one owner exactly 1536 times; every owner is named somewhere. `tile_source`: together with tile_target, every pair of layers s <= t appears exactly once. tile_target[k] >= tile_source[k]. `row_order`: each row is a permutation.
All inputs are finite; a program needn't handle non-finite values.
Results may differ from the reference program's by a relative error of at most 0.0027.
Values may be sent and summed in bfloat16 or wider, within the bound.
A program may use at most 128 MiB of HBM per device.

```python
import math
import jax
import jax.numpy as jnp
import numpy as np
from jax import lax

D = 2304
F = 16384
L = 3
NT = 6
NBLK = 2
TB = 64
TOK = 128
FPD = 1024
CAP = 1536
SLOTS = 12288
N_TILE = 8
N_FEAT = 2


def tile_pairs(key):
    pair_table = np.array([(source, target) for source in range(L) for target in range(source, L)], dtype=np.int32)
    shuffled = jax.random.permutation(jax.random.fold_in(key, 7), pair_table.shape[0])
    return jnp.asarray(pair_table)[shuffled]


def draw_tile_source(key, part):
    return tile_pairs(key)[:, 0].astype(jnp.int32)


def draw_tile_target(key, part):
    return tile_pairs(key)[:, 1].astype(jnp.int32)


def level_of(stream_key, dims, shards, low, high):
    def one(axis_at, blocks):
        steps = jax.random.uniform(jax.random.fold_in(jax.random.fold_in(stream_key, 6), axis_at), (blocks,), jnp.float32, low / len(shards), high / len(shards))
        return jnp.repeat(jnp.exp(steps), dims[axis_at] // blocks).reshape((-1,) + (1,) * (len(dims) - axis_at - 1))

    level = one(*shards[0])
    for cut in shards[1:]:
        level = level * one(*cut)
    return level


def deal_out(rng, own, number, rows, count, top, most, lean):
    order = jax.random.permutation(rng, count)
    heavy_load, usual = portions_of(count, rows * top, most, lean, True), portions_of(count, rows * top, most, lean, False)
    places = jnp.arange(count)

    def named(sizes, offset_by):
        used = int((sizes > 0).sum())
        fixed = max(1, used // 4)
        shifted = fixed + (places - fixed + offset_by * (used - fixed)) % max(1, count - fixed)
        return jnp.zeros((count,), jnp.int32).at[order[jnp.where(places < fixed, places, shifted)]].set(jnp.asarray(sizes, jnp.int32))

    sizes = jnp.where(number % 4 == 0, named(heavy_load, number // 4), named(usual, number - number // 4 - 1))
    mixed = jax.random.permutation(jax.random.fold_in(own, 3), count)
    giver, taker = mixed[0:count // 2 * 2:2], mixed[1:count // 2 * 2:2]
    margin = jnp.minimum(sizes[giver] - 1, most - sizes[taker]) // 2
    margin = jnp.where((giver == order[0]) | (taker == order[0]) | (sizes[taker] == 0), 0, jnp.maximum(margin, 0))
    shifted = jax.random.randint(jax.random.fold_in(own, 4), (count // 2,), 0, 1 << 20) % (margin + 1)
    sizes = sizes.at[giver].add(-shifted).at[taker].add(shifted)
    items = jnp.searchsorted(jnp.cumsum(sizes), jnp.arange(rows * top), side="right").astype(jnp.int32)
    listing = items.reshape(top, rows).T
    listing = listing[jax.random.permutation(jax.random.fold_in(own, 1), rows)]
    offset_by = jax.random.randint(jax.random.fold_in(own, 2), (rows, 1), 0, top)
    return jnp.take_along_axis(listing, (jnp.arange(top)[None, :] + offset_by) % top, axis=1)


def portions_of(count, total, most, lean, full):
    loads = [(1 << 20) // math.isqrt(standing ** lean) + 1 for standing in range(1, count + 1)]
    largest = most if full else min(most, max(-(-total // count), total * loads[0] // sum(loads)))
    least = 1 if total - largest >= count - 1 else 0
    holding, spare = [largest] + [least] * (count - 1), total - largest - least * (count - 1)
    while spare > 0:
        movable = [i for i in range(1, count) if holding[i] < largest] or [i for i in range(1, count) if holding[i] < most]
        mass, left = sum([loads[i] for i in movable]), spare
        for i in movable:
            extra = min(most - holding[i], max(1, left * loads[i] // mass), spare)
            holding[i] = holding[i] + extra
            spare = spare - extra
    return np.array(holding)


def bell_draw(stream_key, dims, scale, limit, cuts=(), kind=jnp.bfloat16):
    values = scale * jax.random.normal(stream_key, dims, jnp.float32)
    if cuts:
        values = values * level_of(stream_key, dims, cuts, -0.22, 0.18)
    return jnp.clip(values, -limit, limit).astype(kind)


def setup_inputs(seed: int = 0, part: int = 0) -> dict:
    key_of = jax.random.split(jax.random.key(seed), 8)
    part_splits = jax.random.split(jax.random.fold_in(key_of[7], part), 8)
    preacts = bell_draw(part_splits[0], (L, F, TOK), 1.0, 6.0, ((1, 16),))
    targets = bell_draw(part_splits[1], (L, 2 * TOK, D // 2), 0.5, 4.0, ((1, 16),))
    decoder = bell_draw(part_splits[2], (N_TILE, N_FEAT, SLOTS, D), (L * F) ** -0.5, 0.02734375, ((0, 8), (1, 2)))
    owner_list_keys = jax.random.split(jax.random.fold_in(key_of[3], 1), F * NT // (NT * FPD))
    owner_list_turns = jax.random.permutation(jax.random.fold_in(key_of[3], 3), F * NT // (NT * FPD))
    owner_list = jax.vmap(lambda own, number: deal_out(jax.random.fold_in(key_of[3], 2), own, number, NT * FPD, N_TILE, 1, CAP, 2))(owner_list_keys, owner_list_turns).reshape((F, NT, 1))
    tile_source = draw_tile_source(jax.random.fold_in(key_of[7], 71), part)
    tile_target = draw_tile_target(jax.random.fold_in(key_of[7], 71), part)
    row_order = jax.vmap(lambda own: jax.random.permutation(own, TB))(jax.random.split(part_splits[6], NBLK)).reshape((NBLK, TB)).astype(jnp.int32)
    return dict(preacts=preacts, targets=targets, decoder=decoder, owner_list=owner_list, tile_source=tile_source, tile_target=tile_target, row_order=row_order)


def reorder(values, indices):
    leading = values.shape[:-1]
    blocks, block_span = indices.shape
    shaped = values.reshape(leading + (blocks, block_span))
    block_col = jnp.arange(blocks, dtype=jnp.int32)[:, None]
    return shaped[..., block_col, indices].reshape(values.shape)


def inverse_order(row_order):
    positions = lax.broadcasted_iota(jnp.int32, row_order.shape, 1)
    block_ids = lax.broadcasted_iota(jnp.int32, row_order.shape, 0)
    inverse = jnp.zeros(row_order.shape, jnp.int32)
    return inverse.at[block_ids, row_order.astype(jnp.int32)].set(positions)


def reference(preacts, targets, decoder, owner_list, tile_source, tile_target, row_order):
    devices_all = N_TILE * N_FEAT
    feat_dev = F // devices_all
    tile_count = tile_source.shape[0]
    active = jax.nn.relu(preacts.astype(jnp.float32)).astype(jnp.bfloat16)
    natural = reorder(active, inverse_order(row_order))
    count_rows = feat_dev * tile_count
    destination = owner_list.reshape(devices_all, count_rows).astype(jnp.int32)
    same_owner = destination[:, :, None] == destination[:, None, :]
    before = lax.broadcasted_iota(jnp.int32, (count_rows, count_rows), 0) < lax.broadcasted_iota(jnp.int32, (count_rows, count_rows), 1)
    slot_rank = jnp.sum((same_owner & before[None]).astype(jnp.int32), axis=1)
    device_ids = lax.broadcasted_iota(jnp.int32, (devices_all, count_rows), 0)
    owner_src = device_ids // N_FEAT
    feat_half = device_ids % N_FEAT
    flat_index = ((destination * N_FEAT + feat_half) * SLOTS + owner_src * CAP + slot_rank).reshape(-1)
    weight_table = decoder.reshape(-1, D)
    row_weights = weight_table[flat_index].reshape(F, tile_count, D)
    layer_ids = jnp.arange(L, dtype=jnp.int32)[:, None, None]
    recon = jnp.zeros((L, TOK, D), jnp.float32)
    for tile_id in range(tile_count):
        product = lax.dot_general(natural[tile_source[tile_id]], row_weights[:, tile_id], (((0,), (0,)), ((), ())), preferred_element_type=jnp.float32)
        recon = recon + jnp.where(layer_ids == tile_target[tile_id], product[None], 0.0)
    residual = recon.reshape(L, 2 * TOK, D // 2) - targets.astype(jnp.float32)
    spread = residual.astype(jnp.bfloat16).reshape(L, TOK, D)
    layer_grad = jnp.zeros((L, F, TOK), jnp.float32)
    for tile_id in range(tile_count):
        product = lax.dot_general(row_weights[:, tile_id], spread[tile_target[tile_id]], (((1,), (1,)), ((), ())), preferred_element_type=jnp.float32)
        layer_grad = layer_grad + jnp.where(layer_ids == tile_source[tile_id], product[None], 0.0)
    natural_pre = reorder(preacts, inverse_order(row_order))
    layer_grad = jnp.where(natural_pre > 0, layer_grad, 0.0)
    return residual, reorder(layer_grad, row_order.astype(jnp.int32))
```

```python
import math

import jax
import jax.numpy as jnp
from jax import lax
from jax.sharding import PartitionSpec as P


def permutation_matrix(row_order):
    blocks, span = row_order.shape
    token = (row_order + span * jnp.arange(blocks, dtype=jnp.int32)[:, None]).reshape(-1)
    ids = lax.broadcasted_iota(jnp.int32, (blocks * span, blocks * span), 1)
    return (token[:, None] == ids).astype(jnp.bfloat16)


def ranks(destination, owners):
    rows = destination.shape[0]
    span = math.gcd(rows, 128)
    blocks = rows // span
    hot = lax.broadcasted_iota(jnp.int32, (owners, rows), 0) == destination[None, :]
    parts = hot.astype(jnp.bfloat16).reshape(owners, blocks, span)

    def earlier(n):
        return (
            lax.broadcasted_iota(jnp.int32, (n, n), 0) < lax.broadcasted_iota(jnp.int32, (n, n), 1)
        ).astype(jnp.bfloat16)

    inner = jnp.dot(parts, earlier(span), preferred_element_type=jnp.float32)
    totals = jnp.sum(parts.astype(jnp.float32), axis=2).astype(jnp.bfloat16)
    outer = jnp.dot(totals, earlier(blocks), preferred_element_type=jnp.float32)
    count = (inner + outer[:, :, None]).reshape(owners, rows)
    return jnp.sum(jnp.where(hot, count, 0.0), axis=0).astype(jnp.int32)


def on_device(preacts, targets, decoder, owner_list, tile_source, tile_target, row_order):
    owners = lax.axis_size("tile")
    layers, feat_dev, tokens = preacts.shape
    tile_count = tile_source.shape[0]
    slot_count = decoder.shape[2]
    capacity = slot_count // owners
    model_width = decoder.shape[3]
    to_token = permutation_matrix(row_order)
    active = jnp.maximum(preacts, jnp.zeros_like(preacts))
    natural = jnp.dot(active, to_token, preferred_element_type=jnp.float32).astype(jnp.bfloat16)
    picked = jnp.zeros((feat_dev, tile_count, tokens), jnp.bfloat16)
    for layer in range(layers):
        picked = jnp.where(
            (tile_source == layer)[None, :, None], natural[layer][:, None, :], picked
        )
    count_rows = feat_dev * tile_count
    row_values = picked.reshape(count_rows, tokens)
    destination = owner_list.reshape(-1)
    slot_of = destination * capacity + ranks(destination, owners)
    tile_of_row = lax.broadcasted_iota(jnp.int32, (feat_dev, tile_count, tokens), 1)
    tile_of_row = (tile_of_row + 1).astype(jnp.bfloat16).reshape(count_rows, tokens)
    slot_match = lax.broadcasted_iota(jnp.int32, (slot_count, count_rows), 0) == slot_of[None, :]
    packed = jnp.dot(
        slot_match.astype(jnp.bfloat16),
        jnp.concatenate([row_values, tile_of_row], axis=1),
        preferred_element_type=jnp.float32,
    ).astype(jnp.bfloat16)
    tile_slot = packed[:, tokens].astype(jnp.int32) - 1
    tile_recv = lax.all_to_all(
        tile_slot.reshape(owners, capacity), "tile", split_axis=0, concat_axis=0, tiled=True
    ).reshape(slot_count)
    received = lax.all_to_all(
        packed[:, :tokens].reshape(owners, capacity, tokens),
        "tile",
        split_axis=0,
        concat_axis=0,
        tiled=True,
    ).reshape(slot_count, tokens)
    tile_ids = lax.broadcasted_iota(jnp.int32, (slot_count, tile_count), 1)
    target_slot = jnp.sum(
        jnp.where(tile_recv[:, None] == tile_ids, tile_target[None, :] + 1, 0), axis=1
    ) - 1
    weights = decoder[0, 0]
    masked = jnp.concatenate(
        [
            jnp.where((target_slot == layer)[:, None], received, jnp.zeros_like(received))
            for layer in range(layers)
        ],
        axis=1,
    )
    partial_value = lax.dot_general(
        masked, weights, (((0,), (0,)), ((), ())), preferred_element_type=jnp.float32
    ).reshape(layers, 2 * tokens, model_width // 2)
    own_sums = lax.psum_scatter(partial_value, ("tile", "feat"), scatter_dimension=1, tiled=True)
    residual = own_sums - targets.astype(jnp.float32)
    spread = lax.all_gather(
        residual.astype(jnp.bfloat16), ("tile", "feat"), axis=1, tiled=True
    ).reshape(layers, tokens, model_width)
    by_column = [
        jnp.dot(to_token, spread[layer], preferred_element_type=jnp.float32).astype(jnp.bfloat16)
        for layer in range(layers)
    ]
    product = lax.dot_general(
        weights,
        jnp.concatenate(by_column, axis=0),
        (((1,), (1,)), ((), ())),
        preferred_element_type=jnp.float32,
    ).astype(jnp.bfloat16)
    slot_grad = jnp.zeros((slot_count, tokens), jnp.bfloat16)
    for layer in range(layers):
        slot_grad = jnp.where(
            (target_slot == layer)[:, None],
            product[:, layer * tokens : (layer + 1) * tokens],
            slot_grad,
        )
    returned = lax.all_to_all(
        slot_grad.reshape(owners, capacity, tokens), "tile", split_axis=0, concat_axis=0, tiled=True
    ).reshape(slot_count, tokens)
    row_grad = returned.astype(jnp.float32)[slot_of].reshape(feat_dev, tile_count, tokens)
    layer_grad = jnp.stack(
        [
            jnp.sum(jnp.where((tile_source == layer)[None, :, None], row_grad, 0.0), axis=1)
            for layer in range(layers)
        ]
    )
    return (residual, jnp.where(preacts > 0, layer_grad, 0.0))


def solution(mesh):
    return jax.shard_map(
        on_device,
        mesh=mesh,
        in_specs=(
            P(None, ("tile", "feat"), "groups"),
            P(None, ("groups", "tile", "feat"), None),
            P(("groups", "tile"), "feat", None, None),
            P(("tile", "feat"), None, None),
            P(),
            P(),
            P("groups", None),
        ),
        out_specs=(P(None, ("groups", "tile", "feat"), None), P(None, ("tile", "feat"), "groups")),
        check_vma=False,
    )
```

```python
import math

import jax
import jax.numpy as jnp
from jax import lax
from jax.sharding import PartitionSpec as P


def permutation_matrix(row_order):
    blocks, span = row_order.shape
    token = (row_order + span * jnp.arange(blocks, dtype=jnp.int32)[:, None]).reshape(-1)
    ids = lax.broadcasted_iota(jnp.int32, (blocks * span, blocks * span), 1)
    return (token[:, None] == ids).astype(jnp.bfloat16)


def ranks(destination, owners):
    rows = destination.shape[0]
    span = math.gcd(rows, 128)
    blocks = rows // span
    hot = lax.broadcasted_iota(jnp.int32, (owners, rows), 0) == destination[None, :]
    parts = hot.astype(jnp.bfloat16).reshape(owners, blocks, span)

    def earlier(n):
        return (
            lax.broadcasted_iota(jnp.int32, (n, n), 0) < lax.broadcasted_iota(jnp.int32, (n, n), 1)
        ).astype(jnp.bfloat16)

    inner = jnp.dot(parts, earlier(span), preferred_element_type=jnp.float32)
    totals = jnp.sum(parts.astype(jnp.float32), axis=2).astype(jnp.bfloat16)
    outer = jnp.dot(totals, earlier(blocks), preferred_element_type=jnp.float32)
    count = (inner + outer[:, :, None]).reshape(owners, rows)
    return jnp.sum(jnp.where(hot, count, 0.0), axis=0).astype(jnp.int32)


def on_device(preacts, targets, decoder, owner_list, tile_source, tile_target, row_order):
    owners = lax.axis_size("tile")
    layers, feat_dev, tokens = preacts.shape
    tile_count = tile_source.shape[0]
    slot_count = decoder.shape[2]
    capacity = slot_count // owners
    model_width = decoder.shape[3]
    to_token = permutation_matrix(row_order)
    active = jnp.maximum(preacts, jnp.zeros_like(preacts))
    natural = jnp.dot(active, to_token, preferred_element_type=jnp.float32).astype(jnp.bfloat16)
    picked = jnp.zeros((feat_dev, tile_count, tokens), jnp.bfloat16)
    for layer in range(layers):
        picked = jnp.where(
            (tile_source == layer)[None, :, None], natural[layer][:, None, :], picked
        )
    count_rows = feat_dev * tile_count
    row_values = picked.reshape(count_rows, tokens)
    destination = owner_list.reshape(-1)
    slot_of = destination * capacity + ranks(destination, owners)
    tile_of_row = lax.broadcasted_iota(jnp.int32, (feat_dev, tile_count, tokens), 1)
    tile_of_row = (tile_of_row + 1).astype(jnp.bfloat16).reshape(count_rows, tokens)
    payload = jnp.concatenate([row_values, tile_of_row], axis=1)
    arrived, arrived_tiles = [], []
    cuts = sorted({0, capacity // 2, capacity})
    for low, high in zip(cuts[:-1], cuts[1:]):
        span = high - low
        owner_id = lax.broadcasted_iota(jnp.int32, (owners, span), 0)
        offset = lax.broadcasted_iota(jnp.int32, (owners, span), 1)
        slot_id = (owner_id * capacity + low + offset).reshape(-1)
        slot_match = slot_id[:, None] == slot_of[None, :]
        packed = jnp.dot(
            slot_match.astype(jnp.bfloat16), payload, preferred_element_type=jnp.float32
        ).astype(jnp.bfloat16)
        arrived.append(
            lax.all_to_all(
                packed[:, :tokens].reshape(owners, span, tokens),
                "tile",
                split_axis=0,
                concat_axis=0,
                tiled=True,
            )
        )
        arrived_tiles.append((packed[:, tokens].astype(jnp.int32) - 1).reshape(owners, span))
    tiles, arrived[0] = lax.optimization_barrier(
        (jnp.concatenate(arrived_tiles, axis=1), arrived[0])
    )
    tile_recv = lax.all_to_all(
        tiles, "tile", split_axis=0, concat_axis=0, tiled=True
    ).reshape(slot_count)
    received = jnp.concatenate(arrived, axis=1).reshape(slot_count, tokens)
    tile_ids = lax.broadcasted_iota(jnp.int32, (slot_count, tile_count), 1)
    target_slot = jnp.sum(
        jnp.where(tile_recv[:, None] == tile_ids, tile_target[None, :] + 1, 0), axis=1
    ) - 1
    weights = decoder[0, 0]
    masked = jnp.concatenate(
        [
            jnp.where((target_slot == layer)[:, None], received, jnp.zeros_like(received))
            for layer in range(layers)
        ],
        axis=1,
    )
    partial_value = lax.dot_general(
        masked, weights, (((0,), (0,)), ((), ())), preferred_element_type=jnp.float32
    ).reshape(layers, 2 * tokens, model_width // 2)
    own_sums = lax.psum_scatter(partial_value, ("tile", "feat"), scatter_dimension=1, tiled=True)
    residual = own_sums - targets.astype(jnp.float32)
    spread = lax.all_gather(
        residual.astype(jnp.bfloat16), ("tile", "feat"), axis=1, tiled=True
    ).reshape(layers, tokens, model_width)
    by_column = [
        jnp.dot(to_token, spread[layer], preferred_element_type=jnp.float32).astype(jnp.bfloat16)
        for layer in range(layers)
    ]
    product = lax.dot_general(
        weights,
        jnp.concatenate(by_column, axis=0),
        (((1,), (1,)), ((), ())),
        preferred_element_type=jnp.float32,
    ).astype(jnp.bfloat16)
    slot_grad = jnp.zeros((slot_count, tokens), jnp.bfloat16)
    for layer in range(layers):
        slot_grad = jnp.where(
            (target_slot == layer)[:, None],
            product[:, layer * tokens : (layer + 1) * tokens],
            slot_grad,
        )
    returned = lax.all_to_all(
        slot_grad.reshape(owners, capacity, tokens), "tile", split_axis=0, concat_axis=0, tiled=True
    ).reshape(slot_count, tokens)
    row_grad = returned.astype(jnp.float32)[slot_of].reshape(feat_dev, tile_count, tokens)
    layer_grad = jnp.stack(
        [
            jnp.sum(jnp.where((tile_source == layer)[None, :, None], row_grad, 0.0), axis=1)
            for layer in range(layers)
        ]
    )
    return (residual, jnp.where(preacts > 0, layer_grad, 0.0))


def solution(mesh):
    return jax.shard_map(
        on_device,
        mesh=mesh,
        in_specs=(
            P(None, ("tile", "feat"), "groups"),
            P(None, ("groups", "tile", "feat"), None),
            P(("groups", "tile"), "feat", None, None),
            P(("tile", "feat"), None, None),
            P(),
            P(),
            P("groups", None),
        ),
        out_specs=(P(None, ("groups", "tile", "feat"), None), P(None, ("tile", "feat"), "groups")),
        check_vma=False,
    )
```

```python
import math

import jax
import jax.numpy as jnp
from jax import lax
from jax.sharding import PartitionSpec as P


def permutation_matrix(row_order):
    blocks, span = row_order.shape
    token = (row_order + span * jnp.arange(blocks, dtype=jnp.int32)[:, None]).reshape(-1)
    ids = lax.broadcasted_iota(jnp.int32, (blocks * span, blocks * span), 1)
    return (token[:, None] == ids).astype(jnp.bfloat16)


def ranks(destination, owners):
    rows = destination.shape[0]
    span = math.gcd(rows, 128)
    blocks = rows // span
    hot = lax.broadcasted_iota(jnp.int32, (owners, rows), 0) == destination[None, :]
    parts = hot.astype(jnp.bfloat16).reshape(owners, blocks, span)

    def earlier(n):
        return (
            lax.broadcasted_iota(jnp.int32, (n, n), 0) < lax.broadcasted_iota(jnp.int32, (n, n), 1)
        ).astype(jnp.bfloat16)

    inner = jnp.dot(parts, earlier(span), preferred_element_type=jnp.float32)
    totals = jnp.sum(parts.astype(jnp.float32), axis=2).astype(jnp.bfloat16)
    outer = jnp.dot(totals, earlier(blocks), preferred_element_type=jnp.float32)
    count = (inner + outer[:, :, None]).reshape(owners, rows)
    return jnp.sum(jnp.where(hot, count, 0.0), axis=0).astype(jnp.int32)


def on_device(preacts, targets, decoder, owner_list, tile_source, tile_target, row_order):
    owners = lax.axis_size("tile")
    layers, feat_dev, tokens = preacts.shape
    tile_count = tile_source.shape[0]
    slot_count = decoder.shape[2]
    capacity = slot_count // owners
    model_width = decoder.shape[3]
    to_token = permutation_matrix(row_order)
    active = jnp.maximum(preacts, jnp.zeros_like(preacts))
    natural = jnp.dot(active, to_token, preferred_element_type=jnp.float32).astype(jnp.bfloat16)
    picked = jnp.zeros((feat_dev, tile_count, tokens), jnp.bfloat16)
    for layer in range(layers):
        picked = jnp.where(
            (tile_source == layer)[None, :, None], natural[layer][:, None, :], picked
        )
    count_rows = feat_dev * tile_count
    row_values = picked.reshape(count_rows, tokens)
    destination = owner_list.reshape(-1)
    slot_of = destination * capacity + ranks(destination, owners)
    tile_of_row = lax.broadcasted_iota(jnp.int32, (feat_dev, tile_count, tokens), 1)
    tile_of_row = (tile_of_row + 1).astype(jnp.bfloat16).reshape(count_rows, tokens)
    payload = jnp.concatenate([row_values, tile_of_row], axis=1)
    arrived, arrived_tiles = [], []
    cuts = sorted({0, capacity // 2, capacity})
    for low, high in zip(cuts[:-1], cuts[1:]):
        span = high - low
        owner_id = lax.broadcasted_iota(jnp.int32, (owners, span), 0)
        offset = lax.broadcasted_iota(jnp.int32, (owners, span), 1)
        slot_id = (owner_id * capacity + low + offset).reshape(-1)
        slot_match = slot_id[:, None] == slot_of[None, :]
        packed = jnp.dot(
            slot_match.astype(jnp.bfloat16), payload, preferred_element_type=jnp.float32
        ).astype(jnp.bfloat16)
        arrived.append(
            lax.all_to_all(
                packed[:, :tokens].reshape(owners, span, tokens),
                "tile",
                split_axis=0,
                concat_axis=0,
                tiled=True,
            )
        )
        arrived_tiles.append((packed[:, tokens].astype(jnp.int32) - 1).reshape(owners, span))
    tiles, arrived[0] = lax.optimization_barrier(
        (jnp.concatenate(arrived_tiles, axis=1), arrived[0])
    )
    tile_recv = lax.all_to_all(
        tiles, "tile", split_axis=0, concat_axis=0, tiled=True
    ).reshape(slot_count)
    received = jnp.concatenate(arrived, axis=1).reshape(slot_count, tokens)
    tile_ids = lax.broadcasted_iota(jnp.int32, (slot_count, tile_count), 1)
    target_slot = jnp.sum(
        jnp.where(tile_recv[:, None] == tile_ids, tile_target[None, :] + 1, 0), axis=1
    ) - 1
    weights = decoder[0, 0]
    masked = jnp.concatenate(
        [
            jnp.where((target_slot == layer)[:, None], received, jnp.zeros_like(received))
            for layer in range(layers)
        ],
        axis=1,
    )
    partial_value = lax.dot_general(
        masked, weights, (((0,), (0,)), ((), ())), preferred_element_type=jnp.float32
    ).reshape(layers, 2 * tokens, model_width // 2)
    own_sums = lax.psum_scatter(partial_value, ("tile", "feat"), scatter_dimension=1, tiled=True)
    residual = own_sums - targets.astype(jnp.float32)
    spread = lax.all_gather(
        residual.astype(jnp.bfloat16), ("tile", "feat"), axis=1, tiled=True
    ).reshape(layers, tokens, model_width)
    by_column = [
        jnp.dot(to_token, spread[layer], preferred_element_type=jnp.float32).astype(jnp.bfloat16)
        for layer in range(layers)
    ]
    columns = jnp.concatenate(by_column, axis=0)
    shaped = weights.reshape(owners, capacity, model_width)
    target_of = target_slot.reshape(owners, capacity)
    pieces = []
    for low, high in zip(cuts[:-1], cuts[1:]):
        product = lax.dot_general(
            shaped[:, low:high],
            columns,
            (((2,), (1,)), ((), ())),
            preferred_element_type=jnp.float32,
        ).astype(jnp.bfloat16)
        slot_grad = jnp.zeros((owners, high - low, tokens), jnp.bfloat16)
        for layer in range(layers):
            slot_grad = jnp.where(
                (target_of[:, low:high] == layer)[:, :, None],
                product[:, :, layer * tokens : (layer + 1) * tokens],
                slot_grad,
            )
        pieces.append(
            lax.all_to_all(slot_grad, "tile", split_axis=0, concat_axis=0, tiled=True)
        )
    returned = jnp.concatenate(pieces, axis=1).reshape(slot_count, tokens)
    row_grad = returned.astype(jnp.float32)[slot_of].reshape(feat_dev, tile_count, tokens)
    layer_grad = jnp.stack(
        [
            jnp.sum(jnp.where((tile_source == layer)[None, :, None], row_grad, 0.0), axis=1)
            for layer in range(layers)
        ]
    )
    return (residual, jnp.where(preacts > 0, layer_grad, 0.0))


def solution(mesh):
    return jax.shard_map(
        on_device,
        mesh=mesh,
        in_specs=(
            P(None, ("tile", "feat"), "groups"),
            P(None, ("groups", "tile", "feat"), None),
            P(("groups", "tile"), "feat", None, None),
            P(("tile", "feat"), None, None),
            P(),
            P(),
            P("groups", None),
        ),
        out_specs=(P(None, ("groups", "tile", "feat"), None), P(None, ("tile", "feat"), "groups")),
        check_vma=False,
    )
```
